256 devices in a mesh: slab: 16 (over z, y_lo), blk: 16 (over y_hi, x, core).
Axes of the slice: x: 4, y: 4 (y_hi: 2, y_lo: 2; y = y_hi * 2 + y_lo), z: 8, core: 2. Of those that a mesh axis runs over, the one named last changes fastest.
Arguments:
- row_emb: float32 [196608, 256], P(('slab', 'blk')), may hold values from -1.5 to 1.5
- col_emb: float32 [196608, 256], P(('slab', 'blk')), may hold values from -1.5 to 1.5
- row_acc: float32 [196608], P(('slab', 'blk')), may hold values from 100000 to 1000000
- col_acc: float32 [196608], P(('slab', 'blk')), may hold values from 100000 to 1000000
- counts: int32 [196608, 4, 768], P(('slab', 'blk')), may hold values from 0 to 1764, as said below
- marginal: int32 [196608], P('slab'), may hold values from 1000 to 90000, as said below
Outputs:
- new_row_emb: float32 [196608, 256], P(('slab', 'blk'))
- new_col_emb: float32 [196608, 256], P(('slab', 'blk'))
- new_row_acc: float32 [196608], P(('slab', 'blk'))
- new_col_acc: float32 [196608], P(('slab', 'blk'))
The draws below stay inside these ranges and needn't reach their ends.
Inputs may be any that keep to these rules, and one draw needn't show every extreme that they name: `counts`: zero or a positive count; some entry equals 1764. Some item has marginal 1000 and some 90000.
All inputs are finite; a program needn't handle non-finite values.
Results may differ from the reference program's by a relative error of at most 0.0075.
Values may be sent and summed in bfloat16 or wider, within the bound.
No kernel may reach another device: no remote copies, remote signals or barrier semaphores. Data moves between devices by JAX's collectives and lax.ppermute only.
A program may use at most 128 MiB of HBM per device.

```python
import math
import jax
import jax.numpy as jnp
from jax import lax

E = 256
B = 768
STEPS = 4
ITEMS = 196608
N_SLAB = 16
N_BLK = 16


def draw_counts(key, part):
    key = jax.random.fold_in(key, 11)
    first_key, second_key, third_key = jax.random.split(key, 3)
    shape = (ITEMS, STEPS, B)
    left = jax.random.randint(first_key, shape, 1, 43)
    right = jax.random.randint(second_key, shape, 1, 43)
    keep = jax.random.randint(third_key, shape, 0, 10) >= 4
    values = jnp.where(keep, left * right, 0).astype(jnp.int32)
    return values.at[0, 0, 0].set(1764)


def draw_marginal(key, part):
    key = jax.random.fold_in(key, 23)
    base_key, slab_key, global_key = jax.random.split(key, 3)
    base = jax.random.randint(base_key, (ITEMS,), 300, 3001)
    position = jnp.arange(ITEMS, dtype=jnp.int32)
    rising = 1024 + 2048 * position // ITEMS
    slab_level = jax.random.randint(slab_key, (N_SLAB,), 1024, 3073)
    global_level = jax.random.randint(global_key, (), 1024, 4097)
    slab_of = position // (B * N_BLK)
    level_row = jnp.sum(jnp.where(slab_of[:, None] == jnp.arange(N_SLAB, dtype=jnp.int32)[None, :], slab_level[None, :], 0), axis=1)
    values = base * rising // 1024
    values = values * level_row // 1024
    values = values * global_level // 1024
    values = jnp.clip(values, 1000, 90000).astype(jnp.int32)
    values = values.at[0].set(1000)
    return values.at[ITEMS - 1].set(90000)


def shard_levels(key, shape, cuts, low, high):
    def one(axis_at, parts):
        draws = jax.random.uniform(jax.random.fold_in(jax.random.fold_in(key, 6), axis_at), (parts,), jnp.float32, low / len(cuts), high / len(cuts))
        return jnp.repeat(jnp.exp(draws), shape[axis_at] // parts).reshape((-1,) + (1,) * (len(shape) - axis_at - 1))

    factor_of = one(*cuts[0])
    for cut in cuts[1:]:
        factor_of = factor_of * one(*cut)
    return factor_of


def scatter_about(own_key, dims, scale, bound, pieces=(), kind=jnp.bfloat16):
    entries = scale * jax.random.normal(own_key, dims, jnp.float32)
    if pieces:
        entries = entries * shard_levels(own_key, dims, pieces, -0.22, 0.18)
    return jnp.clip(entries, -bound, bound).astype(kind)


def setup_inputs(seed: int = 0) -> dict:
    streams_of = jax.random.split(jax.random.key(seed), 7)
    return {
        "row_emb": scatter_about(streams_of[0], (ITEMS, E), 0.25, 1.5, ((0, 256),), jnp.float32),
        "col_emb": scatter_about(streams_of[1], (ITEMS, E), 0.25, 1.5, ((0, 256),), jnp.float32),
        "row_acc": jnp.clip(jnp.exp(math.log(1000000) - 2.3025851 * jax.random.uniform(streams_of[2], (ITEMS,), jnp.float32) ** shard_levels(streams_of[2], (ITEMS,), ((0, 256),), -0.2, 0.2)), 100000.0, 1000000),
        "col_acc": jnp.clip(jnp.exp(math.log(1000000) - 2.3025851 * jax.random.uniform(streams_of[3], (ITEMS,), jnp.float32) ** shard_levels(streams_of[3], (ITEMS,), ((0, 256),), -0.2, 0.2)), 100000.0, 1000000),
        "counts": draw_counts(jax.random.fold_in(streams_of[6], 71), 0),
        "marginal": draw_marginal(jax.random.fold_in(streams_of[6], 71), 0),
    }


learn_rate = 0.5

def tile_gradient(logits, tile_counts, lm_rows, lm_cols, log_total):
    counts_f = tile_counts.astype(jnp.float32)
    target = jnp.log(jnp.maximum(counts_f, 1.0)) + log_total - lm_rows[..., :, None] - lm_cols[..., None, :]
    differ = logits - target
    confidence = 0.1 + 0.25 * jnp.sqrt(counts_f)
    return jnp.where(tile_counts > 0, confidence * differ, jax.nn.sigmoid(differ)).astype(jnp.bfloat16)

def round_back(value):
    return lax.optimization_barrier(value.astype(jnp.bfloat16)).astype(jnp.float32)

def adagrad(params, accum, grads):
    new_accum = accum + lax.optimization_barrier(jnp.mean(grads * grads, axis=-1))
    return (params - learn_rate * grads / jnp.sqrt(new_accum)[..., None], new_accum)

def reference(row_emb, col_emb, row_acc, col_acc, counts, marginal):
    marg_f = marginal.astype(jnp.float32)
    log_total = jnp.log(jnp.sum(marg_f))
    log_marg = jnp.log(marg_f).reshape(N_SLAB, N_BLK, B)
    rows_all = row_emb.reshape(N_SLAB, N_BLK, B, E)
    cols_all = col_emb.reshape(N_SLAB, N_BLK, B, E)
    racc_all = row_acc.reshape(N_SLAB, N_BLK, B)
    cacc_all = col_acc.reshape(N_SLAB, N_BLK, B)
    tiles_all = counts.reshape(N_SLAB, N_BLK, B, STEPS, B)

    def one_slab(packed):
        rows, cols, racc, cacc, tiles, lmarg = packed
        row16 = rows.astype(jnp.bfloat16)
        col16 = cols.astype(jnp.bfloat16)
        row_f = row16.astype(jnp.float32)
        col_f = col16.astype(jnp.float32)
        own_row = jnp.zeros((N_BLK, B, E), jnp.float32)
        own_col = jnp.zeros((N_BLK, B, E), jnp.float32)
        ret_row = jnp.zeros((N_BLK, B, E), jnp.float32)
        ret_col = jnp.zeros((N_BLK, B, E), jnp.float32)
        for offset in range(STEPS):
            shift_by = offset + 1
            row_part = jnp.roll(row_f, shift_by, axis=0)
            col_part = jnp.roll(col_f, shift_by, axis=0)
            lm_part = jnp.roll(lmarg, shift_by, axis=0)
            tile_counts = tiles[:, :, offset, :]
            logit_one = jnp.einsum('bie,bje->bij', row_f, col_part)
            grad_one = tile_gradient(logit_one, tile_counts, lmarg, lm_part, log_total).astype(jnp.float32)
            logit_two = jnp.einsum('bie,bje->bij', col_f, row_part)
            grad_two = tile_gradient(logit_two, tile_counts, lmarg, lm_part, log_total).astype(jnp.float32)
            own_row = own_row + jnp.einsum('bij,bje->bie', grad_one, col_part)
            own_col = own_col + jnp.einsum('bij,bje->bie', grad_two, row_part)
            back_col = jnp.einsum('bij,bie->bje', grad_one, row_f)
            back_row = jnp.einsum('bij,bie->bje', grad_two, col_f)
            ret_row = ret_row + jnp.roll(round_back(back_row), -shift_by, axis=0)
            ret_col = ret_col + jnp.roll(round_back(back_col), -shift_by, axis=0)
        new_rows, new_racc = adagrad(rows, racc, own_row + ret_row)
        new_cols, new_cacc = adagrad(cols, cacc, own_col + ret_col)
        return (new_rows, new_cols, new_racc, new_cacc)
    new_rows, new_cols, new_racc, new_cacc = lax.map(one_slab, (rows_all, cols_all, racc_all, cacc_all, tiles_all, log_marg))
    return (new_rows.reshape(ITEMS, E), new_cols.reshape(ITEMS, E), new_racc.reshape(ITEMS), new_cacc.reshape(ITEMS))
```

```python
import functools

import jax
import jax.numpy as jnp
from jax import lax
from jax.experimental import pallas as pl
from jax.experimental.pallas import tpu as pltpu
from jax.sharding import PartitionSpec as P

learn_rate = 0.5
f32, bf16 = jnp.float32, jnp.bfloat16
VMEM = pl.BlockSpec(memory_space=pltpu.VMEM)
SMEM = pl.BlockSpec(memory_space=pltpu.SMEM)
ANY = pl.BlockSpec(memory_space=pl.ANY)
LARGE = pl.CostEstimate(flops=1 << 37, bytes_accessed=1 << 30, transcendentals=0)
GRANT = 20 << 20
SMALL = pl.CostEstimate(flops=1 << 20, bytes_accessed=1 << 10, transcendentals=0)
RELAY = True
FAR = (768,)


def halves_kernel(row_emb, col_emb, *outs):
    start = 0
    for out in outs:
        span = out.shape[0] // 2
        out[:span, :] = row_emb[pl.ds(start, span), :].astype(bf16)
        out[span:, :] = col_emb[pl.ds(start, span), :].astype(bf16)
        start += span


def rounded(row_emb, col_emb, spans):
    width = row_emb.shape[1]
    return pl.pallas_call(
        halves_kernel,
        in_specs=[VMEM] * 2,
        out_specs=[VMEM] * len(spans),
        out_shape=[jax.ShapeDtypeStruct((2 * span, width), bf16) for span in spans],
        compiler_params=pltpu.CompilerParams(vmem_limit_bytes=8 << 20),
        cost_estimate=SMALL,
        name="rounded",
    )(row_emb, col_emb)


def turned_kernel(row_emb, col_emb, own_half, own_t):
    block, width = row_emb.shape
    for side, emb in enumerate((row_emb, col_emb)):
        values = emb[...].astype(bf16)
        own_half[pl.ds(side * block, block), :] = values * bf16(0.5)
        own_t[pl.ds(side * width, width), :] = values.T


def turned(row_emb, col_emb):
    block, width = row_emb.shape
    return pl.pallas_call(
        turned_kernel,
        in_specs=[VMEM] * 2,
        out_specs=[VMEM] * 2,
        out_shape=[
            jax.ShapeDtypeStruct((2 * block, width), bf16),
            jax.ShapeDtypeStruct((2 * width, block), bf16),
        ],
        compiler_params=pltpu.CompilerParams(vmem_limit_bytes=8 << 20),
        cost_estimate=SMALL,
        name="turned",
    )(row_emb, col_emb)


def lay_kernel(k_ref, counts, *refs):
    outs, held, sems_in, sems_out = refs[:-3], refs[-3], refs[-2], refs[-1]
    copies = [
        pltpu.make_async_copy(counts.at[:, k_ref[i], :], held.at[i], sems_in.at[i])
        for i in range(len(outs))
    ]
    for copy in copies:
        copy.start()
    leaving = []
    for i, out in enumerate(outs):
        copies[i].wait()
        leaving.append(pltpu.make_async_copy(held.at[i], out, sems_out.at[i]))
        leaving[-1].start()
    for copy in leaving:
        copy.wait()


def lay(offsets, counts):
    block, _, width = counts.shape
    steps = len(offsets)
    return pl.pallas_call(
        lay_kernel,
        in_specs=[SMEM, ANY],
        out_specs=[ANY] * steps,
        out_shape=[jax.ShapeDtypeStruct((block, width), jnp.int32)] * steps,
        scratch_shapes=[
            pltpu.VMEM((steps, block, width), jnp.int32),
            pltpu.SemaphoreType.DMA((steps,)),
            pltpu.SemaphoreType.DMA((steps,)),
        ],
        compiler_params=pltpu.CompilerParams(vmem_limit_bytes=56 << 20),
        cost_estimate=SMALL,
        name="lay",
    )(jnp.stack(offsets), counts)


def tile_kernel(
    even_ref, laid, total, more_total, lm_rows, lm_cols, own_half, own_t, *refs,
    start, span, rows, cols, kind,
):
    block = own_half.shape[0] // 2
    width = own_half.shape[1]
    parts = refs[: {"whole": 1, "halves": 2, "either": 3}[kind]]
    acc_in, acc, back_row, back_col, tiles, sems = refs[len(parts) :]
    even = even_ref[0] == 1

    def partner(side, j):
        if kind == "whole":
            return parts[0][pl.ds(side * block + start + j * cols, cols), :]
        if kind == "halves":
            return parts[side][pl.ds(start + j * cols, cols), :]
        return jnp.where(
            even,
            parts[side][pl.ds(start + j * cols, cols), :],
            parts[2][pl.ds(side * block + start + j * cols, cols), :],
        )

    copies = [
        pltpu.make_async_copy(
            laid.at[:, pl.ds(start + j * cols, cols)],
            tiles.at[:, pl.ds(j * cols, cols)],
            sems.at[j],
        )
        for j in range(span // cols)
    ]
    copies[0].start()
    half_log = 0.5 * jnp.log(jnp.sum(total[...] + more_total[...], keepdims=True))
    dims = (((1,), (1,)), ((), ()))
    for j in range(span // cols):
        js = pl.ds(j * cols, cols)
        where = pl.ds(start + j * cols, cols)
        copies[j].wait()
        if j + 1 < len(copies):
            copies[j + 1].start()
        row_part, col_part = partner(0, j), partner(1, j)
        backs = [None, None]
        for i in range(block // rows):
            mine = pl.ds(i * rows, rows)
            seen_counts = tiles[mine, js]
            positive = seen_counts > 0
            safe = jnp.maximum(seen_counts.astype(f32), 1.0)
            goal = 0.5 * jnp.log(safe) + (half_log - 0.5 * lm_rows[mine, :]) - 0.5 * lm_cols[:, where]
            sure = 0.2 + (0.5 * safe) * lax.rsqrt(safe)
            for side, seen in enumerate((col_part, row_part)):
                at = pl.ds(side * block + i * rows, rows)
                logits = lax.dot_general(own_half[at, :], seen, dims, preferred_element_type=f32)
                differ = logits - goal
                grad = jnp.where(positive, sure * differ, 0.5 * jnp.tanh(differ) + 0.5).astype(bf16)
                source = acc_in if j == 0 else acc
                acc[at, :] = source[at, :] + jnp.dot(grad, seen, preferred_element_type=f32)
                more = jnp.dot(
                    own_t[pl.ds(side * width, width), mine], grad, preferred_element_type=f32
                )
                backs[side] = more if backs[side] is None else backs[side] + more
        back_col[:, js] = backs[0].astype(bf16)
        back_row[:, js] = backs[1].astype(bf16)


def tile(even, laid, totals, lm_rows, lm_cols, own_half, own_t, parts, acc, start, span, rows=768, cols=256):
    block, width = own_half.shape[0] // 2, own_half.shape[1]
    cols = min(cols, span)
    kind = ("whole", "halves", "either")[len(parts) - 1]
    return pl.pallas_call(
        functools.partial(tile_kernel, start=start, span=span, rows=rows, cols=cols, kind=kind),
        in_specs=[SMEM, ANY] + [VMEM] * (7 + len(parts)),
        out_specs=[VMEM] * 3,
        out_shape=[jax.ShapeDtypeStruct((2 * block, width), f32)]
        + [jax.ShapeDtypeStruct((width, span), bf16)] * 2,
        scratch_shapes=[
            pltpu.VMEM((block, span), jnp.int32),
            pltpu.SemaphoreType.DMA((span // cols,)),
        ],
        input_output_aliases={8 + len(parts): 0},
        compiler_params=pltpu.CompilerParams(vmem_limit_bytes=GRANT),
        cost_estimate=SMALL,
        name="tile",
    )(even, laid, *totals, lm_rows, lm_cols, own_half, own_t, *parts, acc)


def join_kernel(even_ref, row_here, col_here, row_there, col_there, out):
    width = row_here.shape[0]

    @pl.when(even_ref[0] == 1)
    def _():
        out[:width, :] = row_here[...] + row_there[...]
        out[width:, :] = col_here[...] + col_there[...]

    @pl.when(even_ref[0] != 1)
    def _():
        out[:width, :] = row_there[...]
        out[width:, :] = col_there[...]


def join(even, here, there):
    width, span = here[0].shape
    return pl.pallas_call(
        join_kernel,
        in_specs=[SMEM] + [VMEM] * 4,
        out_specs=VMEM,
        out_shape=jax.ShapeDtypeStruct((2 * width, span), bf16),
        compiler_params=pltpu.CompilerParams(vmem_limit_bytes=8 << 20),
        cost_estimate=SMALL,
        name="join",
    )(even, *here, *there)


def gather_kernel(even_ref, acc, *refs, counts):
    near, chip, out = refs[: counts[0]], refs[counts[0] : -1], refs[-1]
    width = out.shape[0] // 2
    block = out.shape[1]
    even = even_ref[0] == 1
    for half in range(2):
        cut = pl.ds(half * width, width)
        out[cut, :] = acc[pl.ds(half * block, block), :].T
        for pieces, ours in ((near, None), (chip, even)):
            start = 0
            for piece in pieces:
                items = pl.ds(start, piece.shape[1])
                start += piece.shape[1]
                more = piece[cut, :].astype(f32)
                out[cut, items] += more if ours is None else jnp.where(ours, more, 0.0)


def gather_up(even, acc, near, chip):
    width, block = acc.shape[1], acc.shape[0] // 2
    return pl.pallas_call(
        functools.partial(gather_kernel, counts=(len(near), len(chip))),
        in_specs=[SMEM] + [VMEM] * (1 + len(near) + len(chip)),
        out_specs=VMEM,
        out_shape=jax.ShapeDtypeStruct((2 * width, block), f32),
        compiler_params=pltpu.CompilerParams(vmem_limit_bytes=16 << 20),
        cost_estimate=LARGE,
        name="gather_up",
    )(even, acc, *near, *chip)


def update_kernel(even_ref, row_emb, col_emb, row_acc, col_acc, grads, *refs):
    pieces = (len(refs) - 4) // 3
    far, chips = refs[:pieces], refs[pieces:-4]
    even = even_ref[0] == 1
    new_row, new_col, new_racc, new_cacc = refs[-4:]
    block, width = row_emb.shape
    sides = ((row_emb, row_acc, new_row, new_racc), (col_emb, col_acc, new_col, new_cacc))
    for half, (emb, accum, new_emb, new_accum) in enumerate(sides):
        cut = pl.ds(half * width, width)
        start = 0
        for piece, beside in zip(far, chips[half::2]):
            items = pl.ds(start, piece.shape[1])
            start += piece.shape[1]
            grad = grads[cut, items] + piece[cut, :].astype(f32)
            grad += jnp.where(even, beside[...].astype(f32), 0.0)
            total = accum[:, items] + jnp.sum(grad * grad, axis=0, keepdims=True) * (1.0 / width)
            for lane in range(items.start, items.start + items.size, 128):
                new_accum[lane // 128, :] = total[0, lane - items.start : lane - items.start + 128]
            step = grad * (learn_rate * lax.rsqrt(total))
            new_emb[items, :] = emb[items, :] - step.T


def update(even, row_emb, col_emb, row_acc, col_acc, grads, far, chip):
    block, width = row_emb.shape
    return pl.pallas_call(
        update_kernel,
        in_specs=[SMEM] + [VMEM] * (5 + 3 * len(far)),
        out_specs=[VMEM] * 4,
        out_shape=[jax.ShapeDtypeStruct((block, width), f32)] * 2
        + [jax.ShapeDtypeStruct((block // 128, 128), f32)] * 2,
        compiler_params=pltpu.CompilerParams(vmem_limit_bytes=16 << 20),
        cost_estimate=SMALL,
        name="update",
    )(even, row_emb, col_emb, row_acc, col_acc, grads, *far, *chip)


def per_device(row_emb, col_emb, row_acc, col_acc, counts, marginal):
    cycle = lax.axis_size("blk")
    me = lax.axis_index("blk")
    odd = me % 2 == 1
    even = jnp.where(odd, 0, 1).astype(jnp.int32).reshape(1)
    block, width = row_emb.shape

    def moved(array, distance_even, distance_odd=None):
        distance_odd = distance_even if distance_odd is None else distance_odd
        route = [(i, (i + (distance_odd if i % 2 else distance_even)) % cycle) for i in range(cycle)]
        return lax.ppermute(array, "blk", route)

    def swapped(array):
        return moved(array, 1, -1)

    def starts_of(spans):
        return [sum(spans[:i]) for i in range(len(spans))]

    shift_near = jnp.where(odd, 3, 1)
    shift_far = jnp.where(odd, 1, 3)

    marg_f = marginal.astype(f32)
    total = jnp.sum(marg_f.reshape(-1, 8, 128), axis=0)
    slabs = lax.axis_size("slab")

    def from_reach(total, reach):
        return lax.ppermute(total, "slab", [(i, i ^ reach) for i in range(slabs)])

    there = from_reach(total, 1)
    (piece,) = rounded(row_emb, col_emb, (block,))
    near_in = moved(piece, 2)
    shifts = [jnp.int32(2), shift_near, jnp.int32(4), shift_far]
    offsets = [shift - 1 for shift in shifts]
    *first, piece = lax.optimization_barrier((*offsets[:2], piece))
    laid = lay(first, counts)
    *laid, there = lax.optimization_barrier((*laid, there))
    total = total + there
    there = from_reach(total, 2)
    *second, total = lax.optimization_barrier((*offsets[2:], total))
    later = lay(second, counts)
    *later, there = lax.optimization_barrier((*later, there))
    laid = [*laid, *later]
    total = total + there
    there = from_reach(total, 4)
    total = total + there
    there = from_reach(total, 8)
    near_in, total = lax.optimization_barrier((near_in, total))
    far_in = moved(near_in if RELAY else piece, 2 if RELAY else 4)
    row_again, col_again, total = lax.optimization_barrier((row_emb, col_emb, total))
    own_half, own_t = turned(row_again, col_again)
    totals = (total, there)
    log_marg = jnp.log(marg_f).reshape(cycle, 1, block)

    def log_marg_of(place):
        return lax.dynamic_index_in_dim(log_marg, place % cycle, keepdims=False)

    lm_rows = log_marg_of(me).reshape(block, 1)
    acc = jnp.zeros((2 * block, width), f32)
    def tiles(slot, parts, acc, start, span):
        acc, *backs = tile(
            even, laid[slot], totals, lm_rows, log_marg_of(me - shifts[slot]), own_half, own_t, parts,
            acc, start, span,
        )
        return acc, backs

    def both(function, arrays):
        return [function(array) for array in arrays]

    other = swapped(near_in)
    acc, back_two = tiles(0, [near_in], acc, 0, block)
    from_other = both(swapped, back_two)
    acc, back_near = tiles(1, [other], acc, 0, block)
    joined = join(jnp.ones_like(even), back_near, from_other)
    near_out = [moved(joined, -1, -3)]
    acc, joined = lax.optimization_barrier((acc, joined))
    chip_out, far_out = [], []
    to_even = [(i, i - 1) for i in range(1, cycle, 2)]
    to_odd = [(i, i + 1) for i in range(0, cycle, 2)]
    beside = lax.ppermute(piece, "blk", to_odd)
    other = [lax.ppermute(far_in[i * block : (i + 1) * block], "blk", to_even) for i in range(2)]
    for start, span in zip(starts_of(FAR), FAR):
        acc, back_four = tiles(2, [far_in], acc, start, span)
        from_other = both(swapped, back_four)
        acc, back_far = tiles(3, [*other, beside], acc, start, span)
        joined = join(even, back_far, from_other)
        far_out.append(moved(joined, -3, -5))
        acc, joined = lax.optimization_barrier((acc, joined))
        chip_out += both(swapped, back_far)
    grads = gather_up(even, acc, near_out, [])
    new_rows, new_cols, new_racc, new_cacc = update(
        even, row_emb, col_emb, row_acc.reshape(1, block), col_acc.reshape(1, block), grads, far_out, chip_out
    )
    return (new_rows, new_cols, new_racc.reshape(block), new_cacc.reshape(block))


def solution(mesh):
    in_specs = (
        P(("slab", "blk"), None),
        P(("slab", "blk"), None),
        P(("slab", "blk")),
        P(("slab", "blk")),
        P(("slab", "blk"), None, None),
        P("slab"),
    )
    out_specs = (
        P(("slab", "blk"), None),
        P(("slab", "blk"), None),
        P(("slab", "blk")),
        P(("slab", "blk")),
    )
    return jax.shard_map(
        per_device, mesh=mesh, in_specs=in_specs, out_specs=out_specs, check_vma=False
    )
```

```python
import functools

import jax
import jax.numpy as jnp
from jax import lax
from jax.experimental import pallas as pl
from jax.experimental.pallas import tpu as pltpu
from jax.sharding import PartitionSpec as P

learn_rate = 0.5
f32, bf16 = jnp.float32, jnp.bfloat16
VMEM = pl.BlockSpec(memory_space=pltpu.VMEM)
SMEM = pl.BlockSpec(memory_space=pltpu.SMEM)
ANY = pl.BlockSpec(memory_space=pl.ANY)
LARGE = pl.CostEstimate(flops=1 << 37, bytes_accessed=1 << 30, transcendentals=0)
GRANT = 20 << 20
SMALL = pl.CostEstimate(flops=1 << 20, bytes_accessed=1 << 10, transcendentals=0)
RELAY = True
FAR = (768,)


def halves_kernel(row_emb, col_emb, *outs):
    start = 0
    for out in outs:
        span = out.shape[0] // 2
        out[:span, :] = row_emb[pl.ds(start, span), :].astype(bf16)
        out[span:, :] = col_emb[pl.ds(start, span), :].astype(bf16)
        start += span


def rounded(row_emb, col_emb, spans):
    width = row_emb.shape[1]
    return pl.pallas_call(
        halves_kernel,
        in_specs=[VMEM] * 2,
        out_specs=[VMEM] * len(spans),
        out_shape=[jax.ShapeDtypeStruct((2 * span, width), bf16) for span in spans],
        compiler_params=pltpu.CompilerParams(vmem_limit_bytes=8 << 20),
        cost_estimate=SMALL,
        name="rounded",
    )(row_emb, col_emb)


def turned_kernel(row_emb, col_emb, *refs):
    logs, (own_half, own_t, lm_rows), lm_cols = refs[:5], refs[5:8], refs[8:]
    block, width = row_emb.shape
    for side, emb in enumerate((row_emb, col_emb)):
        values = emb[...].astype(bf16)
        own_half[pl.ds(side * block, block), :] = values * bf16(0.5)
        own_t[pl.ds(side * width, width), :] = values.T
    lm_rows[...] = jnp.broadcast_to(logs[0][...], (8, block)).T[:, :1]
    for log, out in zip(logs[1:], lm_cols):
        out[...] = log[...]


def turned(row_emb, col_emb, logs):
    block, width = row_emb.shape
    return pl.pallas_call(
        turned_kernel,
        in_specs=[VMEM] * 7,
        out_specs=[VMEM] * 7,
        out_shape=[
            jax.ShapeDtypeStruct((2 * block, width), bf16),
            jax.ShapeDtypeStruct((2 * width, block), bf16),
            jax.ShapeDtypeStruct((block, 1), f32),
        ]
        + [jax.ShapeDtypeStruct((1, block), f32)] * 4,
        compiler_params=pltpu.CompilerParams(vmem_limit_bytes=12 << 20),
        cost_estimate=SMALL,
        name="turned",
    )(row_emb, col_emb, *logs)


def lay_kernel(k_ref, counts, *refs, base):
    outs, held, sems_in, sems_out = refs[:-3], refs[-3], refs[-2], refs[-1]
    copies = [
        pltpu.make_async_copy(counts.at[:, k_ref[base + i], :], held.at[i], sems_in.at[i])
        for i in range(len(outs))
    ]
    for copy in copies:
        copy.start()
    leaving = []
    for i, out in enumerate(outs):
        copies[i].wait()
        leaving.append(pltpu.make_async_copy(held.at[i], out, sems_out.at[i]))
        leaving[-1].start()
    for copy in leaving:
        copy.wait()


def lay(offsets, counts, base, steps):
    block, _, width = counts.shape
    return pl.pallas_call(
        functools.partial(lay_kernel, base=base),
        in_specs=[SMEM, ANY],
        out_specs=[ANY] * steps,
        out_shape=[jax.ShapeDtypeStruct((block, width), jnp.int32)] * steps,
        scratch_shapes=[
            pltpu.VMEM((steps, block, width), jnp.int32),
            pltpu.SemaphoreType.DMA((steps,)),
            pltpu.SemaphoreType.DMA((steps,)),
        ],
        compiler_params=pltpu.CompilerParams(vmem_limit_bytes=56 << 20),
        cost_estimate=SMALL,
        name="lay",
    )(offsets, counts)


def tile_kernel(
    even_ref, laid, total, more_total, lm_rows, lm_cols, own_half, own_t, *refs,
    start, span, rows, cols, kind, first,
):
    block = own_half.shape[0] // 2
    width = own_half.shape[1]
    parts = refs[: {"whole": 1, "halves": 2, "either": 3}[kind]]
    refs = refs[len(parts) :]
    acc_in, (acc, back_row, back_col, tiles, sems) = (None, refs) if first else (refs[0], refs[1:])
    even = even_ref[0] == 1

    def partner(side, j):
        if kind == "whole":
            return parts[0][pl.ds(side * block + start + j * cols, cols), :]
        if kind == "halves":
            return parts[side][pl.ds(start + j * cols, cols), :]
        return jnp.where(
            even,
            parts[side][pl.ds(start + j * cols, cols), :],
            parts[2][pl.ds(side * block + start + j * cols, cols), :],
        )

    copies = [
        pltpu.make_async_copy(
            laid.at[:, pl.ds(start + j * cols, cols)],
            tiles.at[:, pl.ds(j * cols, cols)],
            sems.at[j],
        )
        for j in range(span // cols)
    ]
    copies[0].start()
    half_log = 0.5 * jnp.log(jnp.sum(total[...] + more_total[...], keepdims=True))
    dims = (((1,), (1,)), ((), ()))
    for j in range(span // cols):
        js = pl.ds(j * cols, cols)
        where = pl.ds(start + j * cols, cols)
        copies[j].wait()
        if j + 1 < len(copies):
            copies[j + 1].start()
        row_part, col_part = partner(0, j), partner(1, j)
        backs = [None, None]
        for i in range(block // rows):
            mine = pl.ds(i * rows, rows)
            seen_counts = tiles[mine, js]
            positive = seen_counts > 0
            safe = jnp.maximum(seen_counts.astype(f32), 1.0)
            goal = 0.5 * jnp.log(safe) + (half_log - 0.5 * lm_rows[mine, :]) - 0.5 * lm_cols[:, where]
            sure = 0.2 + (0.5 * safe) * lax.rsqrt(safe)
            for side, seen in enumerate((col_part, row_part)):
                at = pl.ds(side * block + i * rows, rows)
                logits = lax.dot_general(own_half[at, :], seen, dims, preferred_element_type=f32)
                differ = logits - goal
                grad = jnp.where(positive, sure * differ, 0.5 * jnp.tanh(differ) + 0.5).astype(bf16)
                source = acc_in if j == 0 else acc
                own = jnp.dot(grad, seen, preferred_element_type=f32)
                acc[at, :] = own if source is None else source[at, :] + own
                more = jnp.dot(
                    own_t[pl.ds(side * width, width), mine], grad, preferred_element_type=f32
                )
                backs[side] = more if backs[side] is None else backs[side] + more
        back_col[:, js] = backs[0].astype(bf16)
        back_row[:, js] = backs[1].astype(bf16)


def tile(even, laid, totals, lm_rows, lm_cols, own_half, own_t, parts, acc, start, span, rows=768, cols=256):
    block, width = own_half.shape[0] // 2, own_half.shape[1]
    cols = min(cols, span)
    kind = ("whole", "halves", "either")[len(parts) - 1]
    first = acc is None
    return pl.pallas_call(
        functools.partial(tile_kernel, start=start, span=span, rows=rows, cols=cols, kind=kind, first=first),
        in_specs=[SMEM, ANY] + [VMEM] * (7 - first + len(parts)),
        out_specs=[VMEM] * 3,
        out_shape=[jax.ShapeDtypeStruct((2 * block, width), f32)]
        + [jax.ShapeDtypeStruct((width, span), bf16)] * 2,
        scratch_shapes=[
            pltpu.VMEM((block, span), jnp.int32),
            pltpu.SemaphoreType.DMA((span // cols,)),
        ],
        input_output_aliases={} if first else {8 + len(parts): 0},
        compiler_params=pltpu.CompilerParams(vmem_limit_bytes=GRANT),
        cost_estimate=SMALL,
        name="tile",
    )(even, laid, *totals, lm_rows, lm_cols, own_half, own_t, *parts, *([] if first else [acc]))


def join_kernel(even_ref, row_here, col_here, row_there, col_there, out):
    width = row_here.shape[0]

    @pl.when(even_ref[0] == 1)
    def _():
        out[:width, :] = row_here[...] + row_there[...]
        out[width:, :] = col_here[...] + col_there[...]

    @pl.when(even_ref[0] != 1)
    def _():
        out[:width, :] = row_there[...]
        out[width:, :] = col_there[...]


def join(even, here, there):
    width, span = here[0].shape
    return pl.pallas_call(
        join_kernel,
        in_specs=[SMEM] + [VMEM] * 4,
        out_specs=VMEM,
        out_shape=jax.ShapeDtypeStruct((2 * width, span), bf16),
        compiler_params=pltpu.CompilerParams(vmem_limit_bytes=8 << 20),
        cost_estimate=SMALL,
        name="join",
    )(even, *here, *there)


def gather_kernel(even_ref, acc, *refs, counts):
    near, chip, out = refs[: counts[0]], refs[counts[0] : -1], refs[-1]
    width = out.shape[0] // 2
    block = out.shape[1]
    even = even_ref[0] == 1
    for half in range(2):
        cut = pl.ds(half * width, width)
        out[cut, :] = acc[pl.ds(half * block, block), :].T
        for pieces, ours in ((near, None), (chip, even)):
            start = 0
            for piece in pieces:
                items = pl.ds(start, piece.shape[1])
                start += piece.shape[1]
                more = piece[cut, :].astype(f32)
                out[cut, items] += more if ours is None else jnp.where(ours, more, 0.0)


def gather_up(even, acc, near, chip):
    width, block = acc.shape[1], acc.shape[0] // 2
    return pl.pallas_call(
        functools.partial(gather_kernel, counts=(len(near), len(chip))),
        in_specs=[SMEM] + [VMEM] * (1 + len(near) + len(chip)),
        out_specs=VMEM,
        out_shape=jax.ShapeDtypeStruct((2 * width, block), f32),
        compiler_params=pltpu.CompilerParams(vmem_limit_bytes=16 << 20),
        cost_estimate=LARGE,
        name="gather_up",
    )(even, acc, *near, *chip)


def update_kernel(even_ref, row_emb, col_emb, row_acc, col_acc, grads, *refs):
    pieces = (len(refs) - 4) // 3
    far, chips = refs[:pieces], refs[pieces:-4]
    even = even_ref[0] == 1
    new_row, new_col, new_racc, new_cacc = refs[-4:]
    block, width = row_emb.shape
    sides = ((row_emb, row_acc, new_row, new_racc), (col_emb, col_acc, new_col, new_cacc))
    for half, (emb, accum, new_emb, new_accum) in enumerate(sides):
        cut = pl.ds(half * width, width)
        start = 0
        for piece, beside in zip(far, chips[half::2]):
            items = pl.ds(start, piece.shape[1])
            start += piece.shape[1]
            grad = grads[cut, items] + piece[cut, :].astype(f32)
            grad += jnp.where(even, beside[...].astype(f32), 0.0)
            total = accum[:, items] + jnp.sum(grad * grad, axis=0, keepdims=True) * (1.0 / width)
            for lane in range(items.start, items.start + items.size, 128):
                new_accum[lane // 128, :] = total[0, lane - items.start : lane - items.start + 128]
            step = grad * (learn_rate * lax.rsqrt(total))
            new_emb[items, :] = emb[items, :] - step.T


def update(even, row_emb, col_emb, row_acc, col_acc, grads, far, chip):
    block, width = row_emb.shape
    return pl.pallas_call(
        update_kernel,
        in_specs=[SMEM] + [VMEM] * (5 + 3 * len(far)),
        out_specs=[VMEM] * 4,
        out_shape=[jax.ShapeDtypeStruct((block, width), f32)] * 2
        + [jax.ShapeDtypeStruct((block // 128, 128), f32)] * 2,
        compiler_params=pltpu.CompilerParams(vmem_limit_bytes=16 << 20),
        cost_estimate=SMALL,
        name="update",
    )(even, row_emb, col_emb, row_acc, col_acc, grads, *far, *chip)


def per_device(row_emb, col_emb, row_acc, col_acc, counts, marginal):
    cycle = lax.axis_size("blk")
    me = lax.axis_index("blk")
    odd = me % 2 == 1
    even = jnp.where(odd, 0, 1).astype(jnp.int32).reshape(1)
    block, width = row_emb.shape

    def moved(array, distance_even, distance_odd=None):
        distance_odd = distance_even if distance_odd is None else distance_odd
        route = [(i, (i + (distance_odd if i % 2 else distance_even)) % cycle) for i in range(cycle)]
        return lax.ppermute(array, "blk", route)

    def swapped(array):
        return moved(array, 1, -1)

    def starts_of(spans):
        return [sum(spans[:i]) for i in range(len(spans))]

    shift_near = jnp.where(odd, 3, 1)
    shift_far = jnp.where(odd, 1, 3)

    marg_f = marginal.astype(f32)
    total = jnp.sum(marg_f.reshape(-1, 8, 128), axis=0)
    slabs = lax.axis_size("slab")

    shifts = [jnp.int32(2), shift_near, jnp.int32(4), shift_far]
    offsets = [shift - 1 for shift in shifts]
    offsets = jnp.stack(offsets)

    def from_reach(total, reach):
        return lax.ppermute(total, "slab", [(i, i ^ reach) for i in range(slabs)])

    there = from_reach(total, 1)
    (piece,) = rounded(row_emb, col_emb, (block,))
    near_in = moved(piece, 2)
    to_even = [(i, i - 1) for i in range(1, cycle, 2)]
    to_odd = [(i, i + 1) for i in range(0, cycle, 2)]
    offsets, piece = lax.optimization_barrier((offsets, piece))
    laid = lay(offsets, counts, 0, 2)
    *laid, there = lax.optimization_barrier((*laid, there))
    total = total + there
    there = from_reach(total, 2)
    offsets, total = lax.optimization_barrier((offsets, total))
    beside = lax.ppermute(piece, "blk", to_odd)
    laid += lay(offsets, counts, 2, 2)
    *laid, beside, there = lax.optimization_barrier((*laid, beside, there))
    total = total + there
    there = from_reach(total, 4)
    row_again, col_again, marg_f, total = lax.optimization_barrier((row_emb, col_emb, marg_f, total))
    log_marg = jnp.log(marg_f).reshape(cycle, 1, block)

    def log_marg_of(place):
        return lax.dynamic_index_in_dim(log_marg, place % cycle, keepdims=False)

    logs = [log_marg_of(me)] + [log_marg_of(me - shift) for shift in shifts]
    own_half, own_t, lm_rows, *lm_cols = turned(row_again, col_again, logs)
    own_half, own_t, lm_rows, there, *lm_cols = lax.optimization_barrier(
        (own_half, own_t, lm_rows, there, *lm_cols)
    )
    total = total + there
    there = from_reach(total, 12)
    near_in, there = lax.optimization_barrier((near_in, there))
    far_in = moved(near_in, 2)
    totals = (total, there)

    def tiles(slot, parts, acc, start, span):
        acc, *backs = tile(
            even, laid[slot], totals, lm_rows, lm_cols[slot], own_half, own_t, parts,
            acc, start, span,
        )
        return acc, backs

    def both(function, arrays):
        return [function(array) for array in arrays]

    other = swapped(near_in)
    acc, back_two = tiles(0, [near_in], None, 0, block)
    from_other = both(swapped, back_two)
    acc, back_near = tiles(1, [other], acc, 0, block)
    joined = join(jnp.ones_like(even), back_near, from_other)
    near_out = [moved(joined, -1, -3)]
    acc, joined = lax.optimization_barrier((acc, joined))
    chip_out, far_out = [], []
    other = [lax.ppermute(far_in[i * block : (i + 1) * block], "blk", to_even) for i in range(2)]
    for start, span in zip(starts_of(FAR), FAR):
        acc, back_four = tiles(2, [far_in], acc, start, span)
        from_other = both(swapped, back_four)
        acc, back_far = tiles(3, [*other, beside], acc, start, span)
        joined = join(even, back_far, from_other)
        far_out.append(moved(joined, -3, -5))
        acc, joined = lax.optimization_barrier((acc, joined))
        chip_out += both(swapped, back_far)
    grads = gather_up(even, acc, near_out, [])
    new_rows, new_cols, new_racc, new_cacc = update(
        even, row_emb, col_emb, row_acc.reshape(1, block), col_acc.reshape(1, block), grads, far_out, chip_out
    )
    return (new_rows, new_cols, new_racc.reshape(block), new_cacc.reshape(block))


def solution(mesh):
    in_specs = (
        P(("slab", "blk"), None),
        P(("slab", "blk"), None),
        P(("slab", "blk")),
        P(("slab", "blk")),
        P(("slab", "blk"), None, None),
        P("slab"),
    )
    out_specs = (
        P(("slab", "blk"), None),
        P(("slab", "blk"), None),
        P(("slab", "blk")),
        P(("slab", "blk")),
    )
    return jax.shard_map(
        per_device, mesh=mesh, in_specs=in_specs, out_specs=out_specs, check_vma=False
    )
```

```python
import functools

import jax
import jax.numpy as jnp
from jax import lax
from jax.experimental import pallas as pl
from jax.experimental.pallas import tpu as pltpu
from jax.sharding import PartitionSpec as P

learn_rate = 0.5
f32, bf16 = jnp.float32, jnp.bfloat16
VMEM = pl.BlockSpec(memory_space=pltpu.VMEM)
SMEM = pl.BlockSpec(memory_space=pltpu.SMEM)
ANY = pl.BlockSpec(memory_space=pl.ANY)
LARGE = pl.CostEstimate(flops=1 << 37, bytes_accessed=1 << 30, transcendentals=0)
GRANT = 20 << 20
SMALL = pl.CostEstimate(flops=1 << 20, bytes_accessed=1 << 10, transcendentals=0)
RELAY = True
FAR = (768,)


def halves_kernel(row_emb, col_emb, *outs):
    start = 0
    for out in outs:
        span = out.shape[0] // 2
        out[:span, :] = row_emb[pl.ds(start, span), :].astype(bf16)
        out[span:, :] = col_emb[pl.ds(start, span), :].astype(bf16)
        start += span


def rounded(row_emb, col_emb, spans):
    width = row_emb.shape[1]
    return pl.pallas_call(
        halves_kernel,
        in_specs=[VMEM] * 2,
        out_specs=[VMEM] * len(spans),
        out_shape=[jax.ShapeDtypeStruct((2 * span, width), bf16) for span in spans],
        compiler_params=pltpu.CompilerParams(vmem_limit_bytes=8 << 20),
        cost_estimate=SMALL,
        name="rounded",
    )(row_emb, col_emb)


def turned_kernel(row_emb, col_emb, *refs):
    logs, (own_half, own_t, lm_rows), lm_cols = refs[:5], refs[5:8], refs[8:]
    block, width = row_emb.shape
    for side, emb in enumerate((row_emb, col_emb)):
        values = emb[...].astype(bf16)
        own_half[pl.ds(side * block, block), :] = values * bf16(0.5)
        own_t[pl.ds(side * width, width), :] = values.T
    lm_rows[...] = jnp.broadcast_to(logs[0][...], (8, block)).T[:, :1]
    for log, out in zip(logs[1:], lm_cols):
        out[...] = log[...]


def turned(row_emb, col_emb, logs):
    block, width = row_emb.shape
    return pl.pallas_call(
        turned_kernel,
        in_specs=[VMEM] * 7,
        out_specs=[VMEM] * 7,
        out_shape=[
            jax.ShapeDtypeStruct((2 * block, width), bf16),
            jax.ShapeDtypeStruct((2 * width, block), bf16),
            jax.ShapeDtypeStruct((block, 1), f32),
        ]
        + [jax.ShapeDtypeStruct((1, block), f32)] * 4,
        compiler_params=pltpu.CompilerParams(vmem_limit_bytes=12 << 20),
        cost_estimate=SMALL,
        name="turned",
    )(row_emb, col_emb, *logs)


def lay_kernel(k_ref, counts, *refs, base):
    outs, held, sems_in, sems_out = refs[:-3], refs[-3], refs[-2], refs[-1]
    copies = [
        pltpu.make_async_copy(counts.at[:, k_ref[base + i], :], held.at[i], sems_in.at[i])
        for i in range(len(outs))
    ]
    for copy in copies:
        copy.start()
    leaving = []
    for i, out in enumerate(outs):
        copies[i].wait()
        leaving.append(pltpu.make_async_copy(held.at[i], out, sems_out.at[i]))
        leaving[-1].start()
    for copy in leaving:
        copy.wait()


def lay(offsets, counts, base, steps):
    block, _, width = counts.shape
    return pl.pallas_call(
        functools.partial(lay_kernel, base=base),
        in_specs=[SMEM, ANY],
        out_specs=[ANY] * steps,
        out_shape=[jax.ShapeDtypeStruct((block, width), jnp.int32)] * steps,
        scratch_shapes=[
            pltpu.VMEM((steps, block, width), jnp.int32),
            pltpu.SemaphoreType.DMA((steps,)),
            pltpu.SemaphoreType.DMA((steps,)),
        ],
        compiler_params=pltpu.CompilerParams(vmem_limit_bytes=56 << 20),
        cost_estimate=SMALL,
        name="lay",
    )(offsets, counts)


def tile_kernel(
    even_ref, laid, total, more_total, lm_rows, lm_cols, own_half, own_t, *refs,
    start, span, rows, cols, kind, first,
):
    block = own_half.shape[0] // 2
    width = own_half.shape[1]
    parts = refs[: {"whole": 1, "either": 2}[kind]]
    refs = refs[len(parts) :]
    acc_in, (acc, back_row, back_col, tiles, sems) = (None, refs) if first else (refs[0], refs[1:])
    even = even_ref[0] == 1

    def partner(side, j):
        at = pl.ds(side * block + start + j * cols, cols)
        if kind == "whole":
            return parts[0][at, :]
        return jnp.where(even, parts[0][at, :], parts[1][at, :])

    copies = [
        pltpu.make_async_copy(
            laid.at[:, pl.ds(start + j * cols, cols)],
            tiles.at[:, pl.ds(j * cols, cols)],
            sems.at[j],
        )
        for j in range(span // cols)
    ]
    copies[0].start()
    half_log = 0.5 * jnp.log(jnp.sum(total[...] + more_total[...], keepdims=True))
    dims = (((1,), (1,)), ((), ()))
    for j in range(span // cols):
        js = pl.ds(j * cols, cols)
        where = pl.ds(start + j * cols, cols)
        copies[j].wait()
        if j + 1 < len(copies):
            copies[j + 1].start()
        row_part, col_part = partner(0, j), partner(1, j)
        backs = [None, None]
        for i in range(block // rows):
            mine = pl.ds(i * rows, rows)
            seen_counts = tiles[mine, js]
            positive = seen_counts > 0
            safe = jnp.maximum(seen_counts.astype(f32), 1.0)
            goal = 0.5 * jnp.log(safe) + (half_log - 0.5 * lm_rows[mine, :]) - 0.5 * lm_cols[:, where]
            sure = 0.2 + (0.5 * safe) * lax.rsqrt(safe)
            for side, seen in enumerate((col_part, row_part)):
                at = pl.ds(side * block + i * rows, rows)
                logits = lax.dot_general(own_half[at, :], seen, dims, preferred_element_type=f32)
                differ = logits - goal
                grad = jnp.where(positive, sure * differ, 0.5 * jnp.tanh(differ) + 0.5).astype(bf16)
                source = acc_in if j == 0 else acc
                own = jnp.dot(grad, seen, preferred_element_type=f32)
                acc[at, :] = own if source is None else source[at, :] + own
                more = jnp.dot(
                    own_t[pl.ds(side * width, width), mine], grad, preferred_element_type=f32
                )
                backs[side] = more if backs[side] is None else backs[side] + more
        back_col[:, js] = backs[0].astype(bf16)
        back_row[:, js] = backs[1].astype(bf16)


def tile(even, laid, totals, lm_rows, lm_cols, own_half, own_t, parts, acc, start, span, rows=768, cols=256):
    block, width = own_half.shape[0] // 2, own_half.shape[1]
    cols = min(cols, span)
    kind = ("whole", "either")[len(parts) - 1]
    first = acc is None
    return pl.pallas_call(
        functools.partial(tile_kernel, start=start, span=span, rows=rows, cols=cols, kind=kind, first=first),
        in_specs=[SMEM, ANY] + [VMEM] * (7 - first + len(parts)),
        out_specs=[VMEM] * 3,
        out_shape=[jax.ShapeDtypeStruct((2 * block, width), f32)]
        + [jax.ShapeDtypeStruct((width, span), bf16)] * 2,
        scratch_shapes=[
            pltpu.VMEM((block, span), jnp.int32),
            pltpu.SemaphoreType.DMA((span // cols,)),
        ],
        input_output_aliases={} if first else {8 + len(parts): 0},
        compiler_params=pltpu.CompilerParams(vmem_limit_bytes=GRANT),
        cost_estimate=SMALL,
        name="tile",
    )(even, laid, *totals, lm_rows, lm_cols, own_half, own_t, *parts, *([] if first else [acc]))


def join_kernel(even_ref, row_here, col_here, row_there, col_there, out):
    width = row_here.shape[0]

    @pl.when(even_ref[0] == 1)
    def _():
        out[:width, :] = row_here[...] + row_there[...]
        out[width:, :] = col_here[...] + col_there[...]

    @pl.when(even_ref[0] != 1)
    def _():
        out[:width, :] = row_there[...]
        out[width:, :] = col_there[...]


def join(even, here, there):
    width, span = here[0].shape
    return pl.pallas_call(
        join_kernel,
        in_specs=[SMEM] + [VMEM] * 4,
        out_specs=VMEM,
        out_shape=jax.ShapeDtypeStruct((2 * width, span), bf16),
        compiler_params=pltpu.CompilerParams(vmem_limit_bytes=8 << 20),
        cost_estimate=SMALL,
        name="join",
    )(even, *here, *there)


def gather_kernel(even_ref, acc, *refs, counts):
    near, chip, out = refs[: counts[0]], refs[counts[0] : -1], refs[-1]
    width = out.shape[0] // 2
    block = out.shape[1]
    even = even_ref[0] == 1
    for half in range(2):
        cut = pl.ds(half * width, width)
        out[cut, :] = acc[pl.ds(half * block, block), :].T
        for pieces, ours in ((near, None), (chip, even)):
            start = 0
            for piece in pieces:
                items = pl.ds(start, piece.shape[1])
                start += piece.shape[1]
                more = piece[cut, :].astype(f32)
                out[cut, items] += more if ours is None else jnp.where(ours, more, 0.0)


def gather_up(even, acc, near, chip):
    width, block = acc.shape[1], acc.shape[0] // 2
    return pl.pallas_call(
        functools.partial(gather_kernel, counts=(len(near), len(chip))),
        in_specs=[SMEM] + [VMEM] * (1 + len(near) + len(chip)),
        out_specs=VMEM,
        out_shape=jax.ShapeDtypeStruct((2 * width, block), f32),
        compiler_params=pltpu.CompilerParams(vmem_limit_bytes=16 << 20),
        cost_estimate=LARGE,
        name="gather_up",
    )(even, acc, *near, *chip)


def update_kernel(even_ref, row_emb, col_emb, row_acc, col_acc, grads, *refs):
    pieces = (len(refs) - 4) // 3
    far, chips = refs[:pieces], refs[pieces:-4]
    even = even_ref[0] == 1
    new_row, new_col, new_racc, new_cacc = refs[-4:]
    block, width = row_emb.shape
    sides = ((row_emb, row_acc, new_row, new_racc), (col_emb, col_acc, new_col, new_cacc))
    for half, (emb, accum, new_emb, new_accum) in enumerate(sides):
        cut = pl.ds(half * width, width)
        start = 0
        for piece, beside in zip(far, chips[half::2]):
            items = pl.ds(start, piece.shape[1])
            start += piece.shape[1]
            grad = grads[cut, items] + piece[cut, :].astype(f32)
            grad += jnp.where(even, beside[...].astype(f32), 0.0)
            total = accum[:, items] + jnp.sum(grad * grad, axis=0, keepdims=True) * (1.0 / width)
            for lane in range(items.start, items.start + items.size, 128):
                new_accum[lane // 128, :] = total[0, lane - items.start : lane - items.start + 128]
            step = grad * (learn_rate * lax.rsqrt(total))
            new_emb[items, :] = emb[items, :] - step.T


def update(even, row_emb, col_emb, row_acc, col_acc, grads, far, chip):
    block, width = row_emb.shape
    return pl.pallas_call(
        update_kernel,
        in_specs=[SMEM] + [VMEM] * (5 + 3 * len(far)),
        out_specs=[VMEM] * 4,
        out_shape=[jax.ShapeDtypeStruct((block, width), f32)] * 2
        + [jax.ShapeDtypeStruct((block // 128, 128), f32)] * 2,
        compiler_params=pltpu.CompilerParams(vmem_limit_bytes=16 << 20),
        cost_estimate=SMALL,
        name="update",
    )(even, row_emb, col_emb, row_acc, col_acc, grads, *far, *chip)


def per_device(row_emb, col_emb, row_acc, col_acc, counts, marginal):
    cycle = lax.axis_size("blk")
    me = lax.axis_index("blk")
    odd = me % 2 == 1
    even = jnp.where(odd, 0, 1).astype(jnp.int32).reshape(1)
    block, width = row_emb.shape

    def moved(array, distance_even, distance_odd=None):
        distance_odd = distance_even if distance_odd is None else distance_odd
        route = [(i, (i + (distance_odd if i % 2 else distance_even)) % cycle) for i in range(cycle)]
        return lax.ppermute(array, "blk", route)

    def swapped(array):
        return moved(array, 1, -1)

    def starts_of(spans):
        return [sum(spans[:i]) for i in range(len(spans))]

    shift_near = jnp.where(odd, 3, 1)
    shift_far = jnp.where(odd, 1, 3)

    marg_f = marginal.astype(f32)
    total = jnp.sum(marg_f.reshape(-1, 8, 128), axis=0)
    slabs = lax.axis_size("slab")

    shifts = [jnp.int32(2), shift_near, jnp.int32(4), shift_far]
    offsets = [shift - 1 for shift in shifts]
    offsets = jnp.stack(offsets)

    def from_reach(total, reach):
        return lax.ppermute(total, "slab", [(i, i ^ reach) for i in range(slabs)])

    there = from_reach(total, 1)
    (piece,) = rounded(row_emb, col_emb, (block,))
    near_in = moved(piece, 2)
    to_even = [(i, i - 1) for i in range(1, cycle, 2)]
    to_odd = [(i, i + 1) for i in range(0, cycle, 2)]
    offsets, piece = lax.optimization_barrier((offsets, piece))
    laid = lay(offsets, counts, 0, 2)
    *laid, there = lax.optimization_barrier((*laid, there))
    total = total + there
    there = from_reach(total, 2)
    offsets, total = lax.optimization_barrier((offsets, total))
    beside = lax.ppermute(piece, "blk", to_odd)
    laid += lay(offsets, counts, 2, 2)
    *laid, beside, there = lax.optimization_barrier((*laid, beside, there))
    total = total + there
    there = from_reach(total, 4)
    row_again, col_again, marg_f, total = lax.optimization_barrier((row_emb, col_emb, marg_f, total))
    log_marg = jnp.log(marg_f).reshape(cycle, 1, block)

    def log_marg_of(place):
        return lax.dynamic_index_in_dim(log_marg, place % cycle, keepdims=False)

    logs = [log_marg_of(me)] + [log_marg_of(me - shift) for shift in shifts]
    own_half, own_t, lm_rows, *lm_cols = turned(row_again, col_again, logs)
    own_half, own_t, lm_rows, there, *lm_cols = lax.optimization_barrier(
        (own_half, own_t, lm_rows, there, *lm_cols)
    )
    total = total + there
    there = from_reach(total, 12)
    near_in, there = lax.optimization_barrier((near_in, there))
    far_in = moved(near_in, 2)
    totals = (total, there)

    def tiles(slot, parts, acc, start, span):
        acc, *backs = tile(
            even, laid[slot], totals, lm_rows, lm_cols[slot], own_half, own_t, parts,
            acc, start, span,
        )
        return acc, backs

    def both(function, arrays):
        return [function(array) for array in arrays]

    other = swapped(near_in)
    acc, back_two = tiles(0, [near_in], None, 0, block)
    from_other = both(swapped, back_two)
    acc, back_near = tiles(1, [other], acc, 0, block)
    joined = join(jnp.ones_like(even), back_near, from_other)
    near_out = [moved(joined, -1, -3)]
    acc, joined = lax.optimization_barrier((acc, joined))
    chip_out, far_out = [], []
    other = lax.ppermute(far_in, "blk", to_even)
    for start, span in zip(starts_of(FAR), FAR):
        acc, back_four = tiles(2, [far_in], acc, start, span)
        from_other = both(swapped, back_four)
        acc, back_far = tiles(3, [other, beside], acc, start, span)
        joined = join(even, back_far, from_other)
        far_out.append(moved(joined, -3, -5))
        acc, joined = lax.optimization_barrier((acc, joined))
        chip_out += both(swapped, back_far)
    grads = gather_up(even, acc, near_out, [])
    new_rows, new_cols, new_racc, new_cacc = update(
        even, row_emb, col_emb, row_acc.reshape(1, block), col_acc.reshape(1, block), grads, far_out, chip_out
    )
    return (new_rows, new_cols, new_racc.reshape(block), new_cacc.reshape(block))


def solution(mesh):
    in_specs = (
        P(("slab", "blk"), None),
        P(("slab", "blk"), None),
        P(("slab", "blk")),
        P(("slab", "blk")),
        P(("slab", "blk"), None, None),
        P("slab"),
    )
    out_specs = (
        P(("slab", "blk"), None),
        P(("slab", "blk"), None),
        P(("slab", "blk")),
        P(("slab", "blk")),
    )
    return jax.shard_map(
        per_device, mesh=mesh, in_specs=in_specs, out_specs=out_specs, check_vma=False
    )
```
